256 devices in a mesh: section: 4 (over x), batch: 8 (over y, core), tensor: 8 (over z).
Axes of the slice: x: 4, y: 4, z: 8, core: 2. Of those that a mesh axis runs over, the one named last changes fastest.
Arguments:
- captured: bfloat16 [4096, 3, 8192], P(('section', 'batch'), None, 'tensor'), may hold values from -6 to 6
- fc_weight: bfloat16 [3, 8192, 8192], P(None, 'tensor', ('batch', 'section')), may hold values from -0.0390625 to 0.0390625
- owner: int32 [4096, 1], replicated, may hold values from 0 to 31; in each aligned block of 128 rows (0 to 127, 128 to 255, ...) at most 12 rows name the same one
- norm_gain: float32 [8192], replicated, may hold values from 0.5 to 1.5
Outputs:
- drafted: bfloat16 [32, 8, 4, 12, 8192], P(('section', 'batch'), 'tensor')
The draws below stay inside these ranges and needn't reach their ends.
Inputs may be any that keep to these rules, and one draw needn't show every extreme that they name: In each aligned block of 128 tokens no owner is named more than 12 times, and in some blocks one owner is named exactly 12 times; loads are skewed.
All inputs are finite; a program needn't handle non-finite values.
Results may differ from the reference program's by a relative error of at most 0.0049.
Values may be sent and summed in bfloat16 or wider, within the bound.
No kernel may reach another device: no remote copies, remote signals or barrier semaphores. Data moves between devices by JAX's collectives and lax.ppermute only.
A program may use at most 128 MiB of HBM per device.

```python
import math
import jax
import jax.numpy as jnp
import numpy as np
from jax import lax

D = 8192
TOKENS = 4096
OWNERS = 32
CLASS_ROWS = 128
SLOT_CAP = 12
N_SECTION = 4
N_TENSOR = 8


def levels(key, dims, pieces, least, high):
    def one(axis_at, shards_of):
        heights = jax.random.uniform(jax.random.fold_in(jax.random.fold_in(key, 6), axis_at), (shards_of,), jnp.float32, least / len(pieces), high / len(pieces))
        return jnp.repeat(jnp.exp(heights), dims[axis_at] // shards_of).reshape((-1,) + (1,) * (len(dims) - axis_at - 1))

    level = one(*pieces[0])
    for cut in pieces[1:]:
        level = level * one(*cut)
    return level


def assign_block(key, own, number, rows, amount, top, bound, skew):
    sequence = jax.random.permutation(key, amount)
    crowded, ordinary = load_shares(amount, rows * top, bound, skew, True), load_shares(amount, rows * top, bound, skew, False)
    places = jnp.arange(amount)

    def named(sizes, turn):
        used = int((sizes > 0).sum())
        fixed = max(1, used // 4)
        shifted = fixed + (places - fixed + turn * (used - fixed)) % max(1, amount - fixed)
        return jnp.zeros((amount,), jnp.int32).at[sequence[jnp.where(places < fixed, places, shifted)]].set(jnp.asarray(sizes, jnp.int32))

    sizes = jnp.where(number % 4 == 0, named(crowded, number // 4), named(ordinary, number - number // 4 - 1))
    mixed = jax.random.permutation(jax.random.fold_in(own, 3), amount)
    source_of, taker = mixed[0:amount // 2 * 2:2], mixed[1:amount // 2 * 2:2]
    room = jnp.minimum(sizes[source_of] - 1, bound - sizes[taker]) // 2
    room = jnp.where((source_of == sequence[0]) | (taker == sequence[0]) | (sizes[taker] == 0), 0, jnp.maximum(room, 0))
    shifted = jax.random.randint(jax.random.fold_in(own, 4), (amount // 2,), 0, 1 << 20) % (room + 1)
    sizes = sizes.at[source_of].add(-shifted).at[taker].add(shifted)
    items = jnp.searchsorted(jnp.cumsum(sizes), jnp.arange(rows * top), side="right").astype(jnp.int32)
    listing = items.reshape(top, rows).T
    listing = listing[jax.random.permutation(jax.random.fold_in(own, 1), rows)]
    turn = jax.random.randint(jax.random.fold_in(own, 2), (rows, 1), 0, top)
    return jnp.take_along_axis(listing, (jnp.arange(top)[None, :] + turn) % top, axis=1)


def load_shares(number_of, total, most, lean, full):
    loads = [(1 << 20) // math.isqrt(grade ** lean) + 1 for grade in range(1, number_of + 1)]
    largest = most if full else min(most, max(-(-total // number_of), total * loads[0] // sum(loads)))
    least = 1 if total - largest >= number_of - 1 else 0
    given, surplus = [largest] + [least] * (number_of - 1), total - largest - least * (number_of - 1)
    while surplus > 0:
        candidates = [i for i in range(1, number_of) if given[i] < largest] or [i for i in range(1, number_of) if given[i] < most]
        whole, left = sum([loads[i] for i in candidates]), surplus
        for i in candidates:
            extra = min(most - given[i], max(1, left * loads[i] // whole), surplus)
            given[i] = given[i] + extra
            surplus = surplus - extra
    return np.array(given)


def scatter_about(own_key, dims, spread, limit, split=(), held_as=jnp.bfloat16):
    drawn = jax.random.normal(own_key, dims, jnp.float32) * spread
    if len(split) > 0:
        drawn = levels(own_key, dims, split, -0.22, 0.18) * drawn
    return jnp.clip(drawn, min=-limit, max=limit).astype(held_as)


def setup_inputs(seed: int = 0) -> dict:
    arg_keys = jax.random.split(jax.random.key(seed), 5)
    captured = scatter_about(arg_keys[0], (TOKENS, 3, D), 1.0, 6.0, ((0, 32), (2, 8)))
    fc_weight = scatter_about(arg_keys[1], (3, D, D), (3 * D) ** -0.5, 0.0390625, ((1, 8), (2, 32)))
    owner_keys = jax.random.split(jax.random.fold_in(arg_keys[2], 1), TOKENS // CLASS_ROWS)
    owner_turns = jax.random.permutation(jax.random.fold_in(arg_keys[2], 3), TOKENS // CLASS_ROWS)
    owner = jax.vmap(lambda own, number: assign_block(jax.random.fold_in(arg_keys[2], 2), own, number, CLASS_ROWS, OWNERS, 1, SLOT_CAP, 2))(owner_keys, owner_turns).reshape((TOKENS, 1))
    norm_gain = jnp.clip(1.0 + 0.1 * jax.random.normal(arg_keys[3], (D,), jnp.float32), 0.5, 1.5)
    return dict(captured=captured, fc_weight=fc_weight, owner=owner, norm_gain=norm_gain)


def reference(captured, fc_weight, owner, norm_gain):
    flat_rows = captured.reshape(TOKENS, 3 * D)
    flat_weight = fc_weight.reshape(3 * D, D)
    merged = jnp.dot(flat_rows, flat_weight, preferred_element_type=jnp.float32).astype(jnp.bfloat16)
    values = merged.astype(jnp.float32)
    square_mean = lax.optimization_barrier(jnp.mean(values * values, axis=-1, keepdims=True))
    normed = values * lax.rsqrt(square_mean + 1e-05) * norm_gain
    block_count = N_SECTION * N_TENSOR
    blocks = normed.reshape(block_count, CLASS_ROWS, D)
    block_ids = owner[:, 0].reshape(block_count, CLASS_ROWS)

    def place(pair):
        rows, ids = pair
        onehot = (ids[:, None] == jnp.arange(OWNERS, dtype=jnp.int32)[None, :]).astype(jnp.int32)
        ranks = jnp.cumsum(onehot, axis=0) - 1
        chosen = (ranks[:, :, None] == jnp.arange(SLOT_CAP, dtype=jnp.int32)[None, None, :]) & (onehot[:, :, None] == 1)
        table = chosen.astype(jnp.float32)
        slots = jnp.einsum('rom,rd->omd', table, rows, precision=lax.Precision.HIGHEST)
        return slots.astype(jnp.bfloat16)
    placed = lax.map(place, (blocks, block_ids))
    placed = placed.reshape(N_SECTION, N_TENSOR, OWNERS, SLOT_CAP, D)
    return placed.transpose(2, 1, 0, 3, 4)
```

```python
import jax
import jax.numpy as jnp
from jax import lax
from jax.sharding import PartitionSpec as P

SLOTS_SHARE = 3
F32 = jnp.float32
BF16 = jnp.bfloat16


def shift(value, axis, step):
    n = lax.axis_size(axis)
    return lax.ppermute(value, axis, [(i, (i + step) % n) for i in range(n)])


def hop(value, rows, cores):
    n = lax.axis_size("batch")
    pairs = [(i, ((i // 2 + rows) % (n // 2)) * 2 + (i % 2 ^ cores)) for i in range(n)]
    return lax.ppermute(value, "batch", pairs)


def slot_table(block_ids, owners, slot_cap):
    onehot = (block_ids[..., None] == jnp.arange(owners, dtype=jnp.int32)).astype(jnp.int32)
    ranks = jnp.cumsum(onehot, axis=-2) - 1
    chosen = (ranks[..., None] == jnp.arange(slot_cap, dtype=jnp.int32)) & (onehot[..., None] == 1)
    return chosen.astype(BF16)


def after(value, *earlier):
    return lax.optimization_barrier((value,) + earlier)[0]


def reduce_z(part, place, sign, earlier):
    def block(r):
        return lax.dynamic_index_in_dim(part, place(r), 0, keepdims=False)

    def pair(p, q):
        return jnp.stack([block(p).astype(BF16), block(q).astype(BF16)])

    ahead, behind, last = pair(3 * sign, sign), pair(-3 * sign, -sign), block(4).astype(BF16)
    if earlier:
        ahead, behind, last = after(ahead, *earlier), after(behind, *earlier), after(last, *earlier)
    near = shift(ahead, "tensor", sign).astype(F32)
    far = shift(last, "tensor", 2 * sign).astype(F32)
    back = shift(behind, "tensor", -sign).astype(F32)
    first = (block(2 * sign) + near[0] + far).astype(BF16)
    second = (block(-2 * sign) + back[0]).astype(BF16)
    one = shift(first, "tensor", 2 * sign)
    two = shift(second, "tensor", -2 * sign)
    total = block(0) + (near[1] + back[1]) + (one.astype(F32) + two.astype(F32))
    return total.astype(BF16), (first, second)


def body(captured, fc_weight, owner, norm_gain):
    n_section = lax.axis_size("section")
    n_batch = lax.axis_size("batch")
    n_tensor = lax.axis_size("tensor")
    owners = n_section * n_batch
    rows = captured.shape[0]
    width = norm_gain.shape[0]
    col = fc_weight.shape[2]
    slot_cap = max(2, SLOTS_SHARE * rows // owners)
    si = lax.axis_index("section")
    bi = lax.axis_index("batch")
    ti = lax.axis_index("tensor")
    yi, ci = bi // 2, bi % 2

    own = captured.transpose(1, 0, 2)
    half = col // 2
    w_up = shift(fc_weight, "section", 1)
    w_dn = shift(fc_weight, "section", -1)
    y_up = hop(own, 1, 0)
    y_dn = hop(own, -1, 0)
    sib = hop(own, 0, 1)
    r2 = rows // 2
    far_top = hop(y_up[:, :r2], 1, 0)
    far_bot = hop(y_dn[:, r2:], -1, 0)
    y_up_s = hop(y_up, 0, 1)
    y_dn_s = hop(y_dn, 0, 1)
    far_a = shift(w_up[:, :, :half], "section", 1)
    far_b = shift(w_dn[:, :, half:], "section", -1)
    y_far = jnp.concatenate([far_top, far_bot], axis=1)
    y_far_s = hop(y_far, 0, 1)
    tokens = jnp.concatenate(
        [own, sib, y_dn, y_dn_s, y_far, y_far_s, y_up, y_up_s], axis=1
    )

    def place(r):
        target = (ti + r) % n_tensor
        return ((target // 2 - yi) % (n_batch // 2)) * 2 + (target % 2 ^ ci)

    mine = lax.dynamic_index_in_dim(
        owner[:, 0].reshape(n_section * n_tensor, rows), si * n_tensor + ti, 0, keepdims=False
    )
    table = slot_table(mine, owners, slot_cap)

    def job(weights, sign, earlier):
        weight = jnp.concatenate(weights, axis=2)
        part = jnp.einsum("lnk,lkc->nc", tokens, weight, preferred_element_type=F32)
        part = part.reshape(n_batch, rows, weight.shape[2])
        return reduce_z(part, place, sign, earlier)

    first, _ = job([fc_weight, w_up, w_dn], 1, ())
    second, _ = job([far_a, far_b], -1, ())
    done = [first, second]
    merged = jnp.concatenate(done, axis=1)
    outgoing = jnp.einsum("rom,rc->omc", table, merged, preferred_element_type=F32).astype(BF16)
    incoming = lax.all_to_all(
        outgoing, ("section", "batch"), split_axis=0, concat_axis=0, tiled=True
    )
    incoming = incoming.reshape(n_section, n_batch, slot_cap, n_section, col)
    rows_of = []
    for s in range(n_section):
        order = {(s + d) % n_section: i for i, d in enumerate((0, -1, 1, 2))}
        parts = [incoming[s, :, :, order[p]] for p in range(n_section)]
        rows_of.append(jnp.stack(parts, axis=2).transpose(1, 0, 2, 3).reshape(slot_cap, width))
    values = jnp.stack(rows_of, axis=1).astype(F32)
    square_mean = jnp.mean(values * values, axis=-1, keepdims=True)
    normed = (values * lax.rsqrt(square_mean + 1e-05) * norm_gain).astype(BF16)
    return normed.transpose(1, 0, 2)[None, None]


def solution(mesh):
    return jax.shard_map(
        body,
        mesh=mesh,
        in_specs=(
            P(("section", "batch"), None, "tensor"),
            P(None, "tensor", ("batch", "section")),
            P(),
            P(),
        ),
        out_specs=P(("section", "batch"), "tensor", None, None, None),
        check_vma=False,
    )
```

```python
import jax
import jax.numpy as jnp
from jax import lax
from jax.sharding import PartitionSpec as P

SLOTS_SHARE = 3
F32 = jnp.float32
BF16 = jnp.bfloat16


def shift(value, axis, step):
    n = lax.axis_size(axis)
    return lax.ppermute(value, axis, [(i, (i + step) % n) for i in range(n)])


def hop(value, rows, cores):
    n = lax.axis_size("batch")
    pairs = [(i, ((i // 2 + rows) % (n // 2)) * 2 + (i % 2 ^ cores)) for i in range(n)]
    return lax.ppermute(value, "batch", pairs)


def slot_table(block_ids, owners, slot_cap):
    onehot = (block_ids[..., None] == jnp.arange(owners, dtype=jnp.int32)).astype(jnp.int32)
    ranks = jnp.cumsum(onehot, axis=-2) - 1
    chosen = (ranks[..., None] == jnp.arange(slot_cap, dtype=jnp.int32)) & (onehot[..., None] == 1)
    return chosen.astype(BF16)


def after(value, *earlier):
    return lax.optimization_barrier((value,) + earlier)[0]


def mirror(value, step):
    n_b, n_t = lax.axis_size("batch"), lax.axis_size("tensor")
    pairs = [
        (b * n_t + t, b * n_t + (t + (step if b % 2 == 0 else -step)) % n_t)
        for b in range(n_b)
        for t in range(n_t)
    ]
    return lax.ppermute(value, ("batch", "tensor"), pairs)


def reduce_z(part, place, sign):
    def block(r):
        return lax.dynamic_index_in_dim(part, place(r), 0, keepdims=False)

    def pair(p, q):
        return jnp.stack([block(p).astype(BF16), block(q).astype(BF16)])

    near = mirror(pair(3 * sign, sign), sign).astype(F32)
    far = mirror(block(4).astype(BF16), 2 * sign).astype(F32)
    back = mirror(pair(-3 * sign, -sign), -sign).astype(F32)
    first = (block(2 * sign) + near[0] + far).astype(BF16)
    second = (block(-2 * sign) + back[0]).astype(BF16)
    one = mirror(first, 2 * sign)
    two = mirror(second, -2 * sign)
    total = block(0) + (near[1] + back[1]) + (one.astype(F32) + two.astype(F32))
    return total.astype(BF16)


def body(captured, fc_weight, owner, norm_gain):
    n_section = lax.axis_size("section")
    n_batch = lax.axis_size("batch")
    n_tensor = lax.axis_size("tensor")
    owners = n_section * n_batch
    rows = captured.shape[0]
    width = norm_gain.shape[0]
    col = fc_weight.shape[2]
    slot_cap = max(2, SLOTS_SHARE * rows // owners)
    si = lax.axis_index("section")
    bi = lax.axis_index("batch")
    ti = lax.axis_index("tensor")
    yi, ci = bi // 2, bi % 2

    own = captured.transpose(1, 0, 2)
    half = col // 2
    w_up = shift(fc_weight, "section", 1)
    w_dn = shift(fc_weight, "section", -1)
    y_up = hop(own, 1, 0)
    y_dn = hop(own, -1, 0)
    sib = hop(own, 0, 1)
    r2 = rows // 2
    far_top = hop(y_up[:, :r2], 1, 0)
    far_bot = hop(y_dn[:, r2:], -1, 0)
    y_up_s = hop(y_up, 0, 1)
    y_dn_s = hop(y_dn, 0, 1)
    far_a = shift(w_up[:, :, :half], "section", 1)
    far_b = shift(w_dn[:, :, half:], "section", -1)
    y_far = jnp.concatenate([far_top, far_bot], axis=1)
    y_far_s = hop(y_far, 0, 1)
    tokens = jnp.concatenate(
        [own, sib, y_dn, y_dn_s, y_far, y_far_s, y_up, y_up_s], axis=1
    )

    def place(r):
        target = (ti + r * (1 - 2 * ci)) % n_tensor
        return ((target // 2 - yi) % (n_batch // 2)) * 2 + (target % 2 ^ ci)

    mine = lax.dynamic_index_in_dim(
        owner[:, 0].reshape(n_section * n_tensor, rows), si * n_tensor + ti, 0, keepdims=False
    )
    table = slot_table(mine, owners, slot_cap)

    def job(weights, sign):
        weight = jnp.concatenate(weights, axis=2)
        part = jnp.einsum("lnk,lkc->nc", tokens, weight, preferred_element_type=F32)
        part = part.reshape(n_batch, rows, weight.shape[2])
        return reduce_z(part, place, sign)

    first = job([fc_weight, w_up, w_dn], 1)
    second = job([far_a, far_b], -1)
    done = [first, second]
    here = jnp.concatenate(
        [first[:, :col], first[:, 2 * col :], second, first[:, col : 2 * col]], axis=1
    )
    merged = lax.dynamic_slice_in_dim(
        jnp.concatenate([here, here], axis=1), (n_section - si) % n_section * col, n_section * col, 1
    )
    outgoing = jnp.einsum("rom,rc->omc", table, merged, preferred_element_type=F32).astype(BF16)
    incoming = lax.all_to_all(
        outgoing, ("section", "batch"), split_axis=0, concat_axis=0, tiled=True
    )
    values = incoming.reshape(n_section, n_batch, slot_cap, n_section * col)
    wide = values.astype(F32)
    square_mean = jnp.sum(wide * wide, axis=(1, 3), keepdims=True) / width
    gain = norm_gain.reshape(1, n_batch, 1, n_section * col)
    normed = (wide * lax.rsqrt(square_mean + 1e-05) * gain).astype(BF16)
    return normed.transpose(0, 2, 1, 3).reshape(1, 1, n_section, slot_cap, width)


def solution(mesh):
    return jax.shard_map(
        body,
        mesh=mesh,
        in_specs=(
            P(("section", "batch"), None, "tensor"),
            P(None, "tensor", ("batch", "section")),
            P(),
            P(),
        ),
        out_specs=P(("section", "batch"), "tensor", None, None, None),
        check_vma=False,
    )
```

```python
import jax
import jax.numpy as jnp
from jax import lax
from jax.sharding import PartitionSpec as P

SLOTS_SHARE = 3
F32 = jnp.float32
BF16 = jnp.bfloat16


def shift(value, axis, step):
    n = lax.axis_size(axis)
    return lax.ppermute(value, axis, [(i, (i + step) % n) for i in range(n)])


def hop(value, rows, cores):
    n = lax.axis_size("batch")
    pairs = [(i, ((i // 2 + rows) % (n // 2)) * 2 + (i % 2 ^ cores)) for i in range(n)]
    return lax.ppermute(value, "batch", pairs)


def slot_table(block_ids, owners, slot_cap):
    onehot = (block_ids[..., None] == jnp.arange(owners, dtype=jnp.int32)).astype(jnp.int32)
    ranks = jnp.cumsum(onehot, axis=-2) - 1
    chosen = (ranks[..., None] == jnp.arange(slot_cap, dtype=jnp.int32)) & (onehot[..., None] == 1)
    return chosen.astype(BF16)


def after(value, *earlier):
    return lax.optimization_barrier((value,) + earlier)[0]


def mirror(value, step):
    n_b, n_t = lax.axis_size("batch"), lax.axis_size("tensor")
    pairs = [
        (b * n_t + t, b * n_t + (t + (step if b % 2 == 0 else -step)) % n_t)
        for b in range(n_b)
        for t in range(n_t)
    ]
    return lax.ppermute(value, ("batch", "tensor"), pairs)


def reduce_z(part, place, sign):
    def block(r):
        return lax.dynamic_index_in_dim(part, place(r), 0, keepdims=False)

    def pair(p, q):
        return jnp.stack([block(p).astype(BF16), block(q).astype(BF16)])

    near = mirror(pair(3 * sign, sign), sign).astype(F32)
    far = mirror(block(4).astype(BF16), 2 * sign).astype(F32)
    back = mirror(pair(-3 * sign, -sign), -sign).astype(F32)
    first = (block(2 * sign) + near[0] + far).astype(BF16)
    second = (block(-2 * sign) + back[0]).astype(BF16)
    one = mirror(first, 2 * sign)
    two = mirror(second, -2 * sign)
    total = block(0) + (near[1] + back[1]) + (one.astype(F32) + two.astype(F32))
    return total.astype(BF16)


def body(captured, fc_weight, owner, norm_gain):
    n_section = lax.axis_size("section")
    n_batch = lax.axis_size("batch")
    n_tensor = lax.axis_size("tensor")
    owners = n_section * n_batch
    rows = captured.shape[0]
    width = norm_gain.shape[0]
    col = fc_weight.shape[2]
    slot_cap = max(2, SLOTS_SHARE * rows // owners)
    si = lax.axis_index("section")
    bi = lax.axis_index("batch")
    ti = lax.axis_index("tensor")
    yi, ci = bi // 2, bi % 2

    own = captured.transpose(1, 0, 2)
    half = col // 2
    w_up = shift(fc_weight, "section", 1)
    w_dn = shift(fc_weight, "section", -1)
    y_up = hop(own, 1, 0)
    y_dn = hop(own, -1, 0)
    sib = hop(own, 0, 1)
    r2 = rows // 2
    far_top = hop(y_up[:, :r2], 1, 0)
    far_bot = hop(y_dn[:, r2:], -1, 0)
    y_up_s = hop(y_up, 0, 1)
    y_dn_s = hop(y_dn, 0, 1)
    far_a = shift(w_up[:, :, :half], "section", 1)
    far_b = shift(w_dn[:, :, half:], "section", -1)
    y_far = jnp.concatenate([far_top, far_bot], axis=1)
    y_far_s = hop(y_far, 0, 1)
    tokens = jnp.concatenate(
        [own, sib, y_dn, y_dn_s, y_far, y_far_s, y_up, y_up_s], axis=1
    )

    def place(r):
        target = (ti + r * (1 - 2 * ci)) % n_tensor
        return ((target // 2 - yi) % (n_batch // 2)) * 2 + (target % 2 ^ ci)

    mine = lax.dynamic_index_in_dim(
        owner[:, 0].reshape(n_section * n_tensor, rows), si * n_tensor + ti, 0, keepdims=False
    )
    table = slot_table(mine, owners, slot_cap)

    def job(weights, sign):
        weight = jnp.concatenate(weights, axis=2)
        part = jnp.einsum("lnk,lkc->nc", tokens, weight, preferred_element_type=F32)
        part = part.reshape(n_batch, rows, weight.shape[2])
        return reduce_z(part, place, sign)

    first = job([fc_weight, w_up, w_dn], 1)
    second = job([far_a, far_b], -1)
    done = [first, second]
    here = jnp.concatenate(
        [first[:, :col], first[:, 2 * col :], second, first[:, col : 2 * col]], axis=1
    )
    merged = lax.dynamic_slice_in_dim(
        jnp.concatenate([here, here], axis=1), (n_section - si) % n_section * col, n_section * col, 1
    )
    outgoing = jnp.einsum("rom,rc->omc", table, merged, preferred_element_type=F32).astype(BF16)
    outgoing = outgoing.reshape(owners, slot_cap // 4, 4, n_section * col)
    incoming = lax.all_to_all(
        outgoing, ("section", "batch"), split_axis=0, concat_axis=0, tiled=True
    )
    values = incoming.reshape(n_section, n_batch, slot_cap // 4, 4, n_section * col)
    wide = values.astype(F32)
    square_mean = jnp.sum(wide * wide, axis=(1, 4), keepdims=True) / width
    gain = norm_gain.reshape(1, n_batch, 1, 1, n_section * col)
    normed = (wide * lax.rsqrt(square_mean + 1e-05) * gain).astype(BF16)
    return normed.transpose(0, 2, 3, 1, 4).reshape(1, 1, n_section, slot_cap, width)


def solution(mesh):
    return jax.shard_map(
        body,
        mesh=mesh,
        in_specs=(
            P(("section", "batch"), None, "tensor"),
            P(None, "tensor", ("batch", "section")),
            P(),
            P(),
        ),
        out_specs=P(("section", "batch"), "tensor", None, None, None),
        check_vma=False,
    )
```

```python
import jax
import jax.numpy as jnp
from jax import lax
from jax.sharding import PartitionSpec as P

SLOTS_SHARE = 3
F32 = jnp.float32
BF16 = jnp.bfloat16


def shift(value, axis, step):
    n = lax.axis_size(axis)
    return lax.ppermute(value, axis, [(i, (i + step) % n) for i in range(n)])


def hop(value, rows, cores):
    n = lax.axis_size("batch")
    pairs = [(i, ((i // 2 + rows) % (n // 2)) * 2 + (i % 2 ^ cores)) for i in range(n)]
    return lax.ppermute(value, "batch", pairs)


def slot_table(block_ids, owners, slot_cap):
    onehot = (block_ids[..., None] == jnp.arange(owners, dtype=jnp.int32)).astype(jnp.int32)
    ranks = jnp.cumsum(onehot, axis=-2) - 1
    chosen = (ranks[..., None] == jnp.arange(slot_cap, dtype=jnp.int32)) & (onehot[..., None] == 1)
    return chosen.astype(BF16)


def after(value, *earlier):
    return lax.optimization_barrier((value,) + earlier)[0]


def mirror(value, step):
    n_b, n_t = lax.axis_size("batch"), lax.axis_size("tensor")
    pairs = [
        (b * n_t + t, b * n_t + (t + (step if b % 2 == 0 else -step)) % n_t)
        for b in range(n_b)
        for t in range(n_t)
    ]
    return lax.ppermute(value, ("batch", "tensor"), pairs)


def reduce_z(part, place, sign):
    def block(r):
        return lax.dynamic_index_in_dim(part, place(r), 0, keepdims=False)

    def pair(p, q):
        return jnp.stack([block(p).astype(BF16), block(q).astype(BF16)])

    near = mirror(pair(3 * sign, sign), sign).astype(F32)
    far = mirror(block(4).astype(BF16), 2 * sign).astype(F32)
    back = mirror(pair(-3 * sign, -sign), -sign).astype(F32)
    first = (block(2 * sign) + near[0] + far).astype(BF16)
    second = (block(-2 * sign) + back[0]).astype(BF16)
    one = mirror(first, 2 * sign)
    two = mirror(second, -2 * sign)
    total = block(0) + (near[1] + back[1]) + (one.astype(F32) + two.astype(F32))
    return total.astype(BF16)


def relay(up, down, core, axes):
    n_s, n_b = lax.axis_size("section"), lax.axis_size("batch")
    pairs = []
    for s in range(n_s):
        for b in range(n_b):
            step = 1 if b % 2 == 0 else -1
            if axes == "section":
                to = ((s + step) % n_s) * n_b + b
            else:
                to = s * n_b + ((b // 2 + step) % (n_b // 2)) * 2 + b % 2
            pairs.append((s * n_b + b, to))
    return lax.ppermute(jnp.where(core == 0, up, down), ("section", "batch"), pairs)


def body(captured, fc_weight, owner, norm_gain):
    n_section = lax.axis_size("section")
    n_batch = lax.axis_size("batch")
    n_tensor = lax.axis_size("tensor")
    owners = n_section * n_batch
    rows = captured.shape[0]
    width = norm_gain.shape[0]
    col = fc_weight.shape[2]
    slot_cap = max(2, SLOTS_SHARE * rows // owners)
    si = lax.axis_index("section")
    bi = lax.axis_index("batch")
    ti = lax.axis_index("tensor")
    yi, ci = bi // 2, bi % 2

    own = captured.transpose(1, 0, 2)
    w_up = shift(fc_weight, "section", 1)
    w_dn = shift(fc_weight, "section", -1)
    y_up = hop(own, 1, 0)
    y_dn = hop(own, -1, 0)
    sib = hop(own, 0, 1)
    y_far = relay(y_up, y_dn, ci, "batch")
    y_up_s = hop(y_up, 0, 1)
    y_dn_s = hop(y_dn, 0, 1)
    w_far = relay(w_up, w_dn, ci, "section")
    y_far_s = hop(y_far, 0, 1)
    tokens = jnp.concatenate(
        [own, sib, y_dn, y_dn_s, y_far, y_far_s, y_up, y_up_s], axis=1
    )

    def place(r):
        target = (ti + r * (1 - 2 * ci)) % n_tensor
        return ((target // 2 - yi) % (n_batch // 2)) * 2 + (target % 2 ^ ci)

    mine = lax.dynamic_index_in_dim(
        owner[:, 0].reshape(n_section * n_tensor, rows), si * n_tensor + ti, 0, keepdims=False
    )
    table = slot_table(mine, owners, slot_cap)

    def job(weights, sign):
        weight = jnp.concatenate(weights, axis=2)
        part = jnp.einsum("lnk,lkc->nc", tokens, weight, preferred_element_type=F32)
        part = part.reshape(n_batch, rows, weight.shape[2])
        return reduce_z(part, place, sign)

    first = job([fc_weight, w_up, w_dn], 1)
    second = job([w_far], -1)
    done = [first, second]
    here = jnp.concatenate(
        [first[:, :col], first[:, 2 * col :], second, first[:, col : 2 * col]], axis=1
    )
    merged = lax.dynamic_slice_in_dim(
        jnp.concatenate([here, here], axis=1), (n_section - si) % n_section * col, n_section * col, 1
    )
    outgoing = jnp.einsum("rom,rc->omc", table, merged, preferred_element_type=F32).astype(BF16)
    outgoing = outgoing.reshape(owners, slot_cap // 4, 4, n_section * col)
    incoming = lax.all_to_all(
        outgoing, ("section", "batch"), split_axis=0, concat_axis=0, tiled=True
    )
    values = incoming.reshape(n_section, n_batch, slot_cap // 4, 4, n_section * col)
    wide = values.astype(F32)
    square_mean = jnp.sum(wide * wide, axis=(1, 4), keepdims=True) / width
    gain = norm_gain.reshape(1, n_batch, 1, 1, n_section * col)
    normed = (wide * lax.rsqrt(square_mean + 1e-05) * gain).astype(BF16)
    return normed.transpose(0, 2, 3, 1, 4).reshape(1, 1, n_section, slot_cap, width)


def solution(mesh):
    return jax.shard_map(
        body,
        mesh=mesh,
        in_specs=(
            P(("section", "batch"), None, "tensor"),
            P(None, "tensor", ("batch", "section")),
            P(),
            P(),
        ),
        out_specs=P(("section", "batch"), "tensor", None, None, None),
        check_vma=False,
    )
```
